32 devices in a mesh: clips: 2 (over y), tm: 4 (over x, core), rows: 4 (over z).
Axes of the slice: x: 2, y: 2, z: 4, core: 2. Of those that a mesh axis runs over, the one named last changes fastest.
Arguments:
- features: bfloat16 [8, 8, 48, 384], P(('clips', 'tm'), 'rows'), parts along dimension 0, may hold values from -320 to 320
- first_gain: float32 [384], replicated, may hold values from 0.5 to 1.5
- first_shift: float32 [384], replicated, may hold values from -3 to 3
- first_kernel: bfloat16 [384, 3, 3, 3, 384], P('tm'), may hold values from -0.0625 to 0.0625
- first_bias: float32 [384], P('tm'), may hold values from -2 to 2
- second_gain: float32 [384], replicated, may hold values from 0.5 to 1.5
- second_shift: float32 [384], replicated, may hold values from -3 to 3
- second_kernel: bfloat16 [384, 3, 3, 3, 384], P('tm'), may hold values from -0.0625 to 0.0625
- second_bias: float32 [384], P('tm'), may hold values from -2 to 2
- third_gain: float32 [384], replicated, may hold values from 0.5 to 1.5
- third_shift: float32 [384], replicated, may hold values from -3 to 3
- query_weight: bfloat16 [384, 384], replicated, may hold values from -0.30618622 to 0.30618622
- key_weight: bfloat16 [384, 384], replicated, may hold values from -1.8371173 to 1.8371173
- value_weight: bfloat16 [384, 384], replicated, may hold values from -0.3125 to 0.3125
- output_weight: bfloat16 [384, 384], replicated, may hold values from -0.3125 to 0.3125
Outputs:
- decoded: bfloat16 [8, 8, 48, 384], P(('clips', 'tm'), 'rows'), parts along dimension 0
The draws below stay inside these ranges and needn't reach their ends.
There are 2 independent parts, one for each index of `clips`. The reference program is written for one: setup_inputs(seed, part) draws one part's arguments, and reference() takes and returns one part's arrays. A program takes and returns all parts, laid end to end along the dimension named above; an argument that names none is the same for every part. Nothing has to cross between parts.
All inputs are finite; a program needn't handle non-finite values.
Results may differ from the reference program's by a relative error of at most 0.029.
Values may be sent and summed in bfloat16 or wider, within the bound.
A program may use at most 64 MiB of HBM per device.

```python
import jax
import jax.numpy as jnp
from jax import lax

C = 384
GROUPS = 32
WIDTH = 48
HEIGHT = 8
FRAMES = 4


def draw_features(key, part):
    base = jnp.clip(jax.random.normal(jax.random.fold_in(key, 1), (FRAMES, HEIGHT, WIDTH, C), jnp.float32), -6.0, 6.0)
    ramp = jnp.arange(HEIGHT, dtype=jnp.float32) / max(HEIGHT - 1, 1)
    rough = jnp.exp(jax.random.uniform(jax.random.fold_in(key, 3), (HEIGHT,), jnp.float32) * jnp.log(20.0)) / 20.0
    level = ((1.0 + 2.0 * ramp) * rough)[None, :, None, None]
    value = 0.5 * base * level
    return jnp.clip(value, -320.0, 320.0).astype(jnp.bfloat16)


def attention_pair(key):
    first = jnp.clip(jax.random.normal(jax.random.fold_in(key, 11), (C, C), jnp.float32), -6.0, 6.0) * C ** (-0.5)
    noise = jnp.clip(jax.random.normal(jax.random.fold_in(key, 12), (C, C), jnp.float32), -6.0, 6.0) * C ** (-0.5)
    second = noise
    return (first, second)


def draw_query_weight(key, part):
    return attention_pair(key)[0].astype(jnp.bfloat16)


def draw_key_weight(key, part):
    return attention_pair(key)[1].astype(jnp.bfloat16)


def levels(stream_key, shape, split, smallest, high):
    loudness, own = 1.0, jax.random.fold_in(stream_key, 6)
    for axis_at, shards_of in split:
        heights = jnp.exp(jax.random.uniform(jax.random.fold_in(own, axis_at), (shards_of,), jnp.float32, smallest / len(split), high / len(split)))
        loudness = loudness * jnp.repeat(heights, shape[axis_at] // shards_of).reshape([-1 if axis == axis_at else 1 for axis in range(len(shape))])
    return loudness


def normal_values(key, dims, scale, reach, pieces=(), held_as=jnp.bfloat16):
    factor_of = levels(key, dims, pieces, -0.22, 0.18) if pieces else 1.0
    result = jax.random.normal(key, dims, jnp.float32) * scale * factor_of
    return jnp.minimum(jnp.maximum(result, -reach), reach).astype(held_as)


def setup_inputs(seed: int = 0, part: int = 0) -> dict:
    key_list = jax.random.split(jax.random.key(seed), 16)
    part_splits = jax.random.split(jax.random.fold_in(key_list[15], part), 16)
    return {
        "features": draw_features(jax.random.fold_in(jax.random.fold_in(key_list[15], part), 71), part),
        "first_gain": jnp.clip(1.0 + 0.1 * jax.random.normal(key_list[1], (C,), jnp.float32), 0.5, 1.5),
        "first_shift": normal_values(key_list[2], (C,), 0.5, 3.0, (), jnp.float32),
        "first_kernel": normal_values(key_list[3], (C, 3, 3, 3, C), (27 * C) ** -0.5, 0.0625, ((0, 4),)),
        "first_bias": normal_values(key_list[4], (C,), 0.3, 2.0, ((0, 4),), jnp.float32),
        "second_gain": jnp.clip(1.0 + 0.1 * jax.random.normal(key_list[5], (C,), jnp.float32), 0.5, 1.5),
        "second_shift": normal_values(key_list[6], (C,), 0.5, 3.0, (), jnp.float32),
        "second_kernel": normal_values(key_list[7], (C, 3, 3, 3, C), (27 * C) ** -0.5, 0.0625, ((0, 4),)),
        "second_bias": normal_values(key_list[8], (C,), 0.3, 2.0, ((0, 4),), jnp.float32),
        "third_gain": jnp.clip(1.0 + 0.1 * jax.random.normal(key_list[9], (C,), jnp.float32), 0.5, 1.5),
        "third_shift": normal_values(key_list[10], (C,), 0.5, 3.0, (), jnp.float32),
        "query_weight": draw_query_weight(jax.random.fold_in(key_list[15], 71), part),
        "key_weight": draw_key_weight(jax.random.fold_in(key_list[15], 71), part),
        "value_weight": normal_values(key_list[13], (C, C), C ** -0.5, 0.3125),
        "output_weight": normal_values(key_list[14], (C, C), C ** -0.5, 0.3125),
    }


epsilon = 1e-06

def group_norm(values, gain, shift):
    frame_count, row_count, col_count, channels = values.shape
    grouped = values.reshape(frame_count, row_count, col_count, GROUPS, channels // GROUPS)
    average = lax.optimization_barrier(jnp.mean(grouped, axis=(1, 2, 4), keepdims=True))
    variance = lax.optimization_barrier(jnp.mean(jnp.square(grouped - average), axis=(1, 2, 4), keepdims=True))
    normal_part = ((grouped - average) / jnp.sqrt(variance + epsilon)).reshape(frame_count, row_count, col_count, channels)
    return normal_part * gain + shift

def causal_conv(active, kernel, bias):
    frame_count, row_count, col_count, channels = active.shape
    outputs = kernel.shape[0]
    padded = jnp.pad(active, ((2, 0), (1, 1), (1, 1), (0, 0)))
    summed = jnp.zeros((frame_count * row_count * col_count, outputs), jnp.float32)
    for tap_time in range(3):
        for tap_row in range(3):
            window = padded[tap_time:tap_time + frame_count, tap_row:tap_row + row_count]
            stacked = jnp.concatenate([window[:, :, shift_col:shift_col + col_count] for shift_col in range(3)], axis=-1)
            tap_weight = kernel[:, tap_time, tap_row].reshape(outputs, 3 * channels)
            summed = summed + lax.dot_general(stacked.reshape(-1, 3 * channels), tap_weight, (((1,), (1,)), ((), ())), preferred_element_type=jnp.float32)
    summed = summed + bias
    return summed.reshape(frame_count, row_count, col_count, -1).astype(jnp.bfloat16)

def frame_attention(inputs):
    queries, keys, values = inputs
    scores = jnp.dot(queries, keys.T, preferred_element_type=jnp.float32)
    peak = lax.optimization_barrier(jnp.max(scores, axis=-1, keepdims=True))
    expon = jnp.exp(scores - peak)
    total = lax.optimization_barrier(jnp.sum(expon, axis=-1, keepdims=True))
    summed = jnp.dot(expon.astype(jnp.bfloat16), values, preferred_element_type=jnp.float32)
    return (summed / total).astype(jnp.bfloat16)

def reference(features, first_gain, first_shift, first_kernel, first_bias, second_gain, second_shift, second_kernel, second_bias, third_gain, third_shift, query_weight, key_weight, value_weight, output_weight):
    frame_count, row_count, col_count, channels = features.shape
    start = features.astype(jnp.float32)
    active1 = jax.nn.silu(group_norm(start, first_gain, first_shift)).astype(jnp.bfloat16)
    conv1 = causal_conv(active1, first_kernel, first_bias)
    active2 = jax.nn.silu(group_norm(conv1.astype(jnp.float32), second_gain, second_shift)).astype(jnp.bfloat16)
    conv2 = causal_conv(active2, second_kernel, second_bias)
    hidden = (start + conv2.astype(jnp.float32)).astype(jnp.bfloat16)
    normed = group_norm(hidden.astype(jnp.float32), third_gain, third_shift).astype(jnp.bfloat16)
    flat = normed.reshape(-1, channels)
    queries = (jnp.dot(flat, query_weight, preferred_element_type=jnp.float32) * C ** (-0.5)).astype(jnp.bfloat16)
    keys = jnp.dot(flat, key_weight, preferred_element_type=jnp.float32).astype(jnp.bfloat16)
    values = jnp.dot(flat, value_weight, preferred_element_type=jnp.float32).astype(jnp.bfloat16)
    shape3 = (frame_count, row_count * col_count, channels)
    attended = lax.map(frame_attention, (queries.reshape(shape3), keys.reshape(shape3), values.reshape(shape3)))
    projected = jnp.dot(attended.reshape(-1, channels), output_weight, preferred_element_type=jnp.float32)
    decoded = hidden.astype(jnp.float32).reshape(-1, channels) + projected
    return decoded.astype(jnp.bfloat16).reshape(frame_count, row_count, col_count, channels)
```

```python
import functools

import jax
import jax.numpy as jnp
from jax import lax
from jax.experimental import pallas as pl
from jax.experimental.pallas import tpu as pltpu
from jax.sharding import PartitionSpec as P

GROUPS = 32
EPS = 1e-06
LANES = 128
MESH = pl.DeviceIdType.MESH
F32 = jnp.float32
BF16 = jnp.bfloat16
NT = (((1,), (1,)), ((), ()))


def each(count, body):
    if count <= 16:
        for n in range(count):
            body(n)
    else:
        lax.fori_loop(0, count, lambda n, c: (body(n), c)[1], 0)


def membership(size, per_group):
    a = lax.broadcasted_iota(jnp.int32, (size, size), 0) // per_group
    b = lax.broadcasted_iota(jnp.int32, (size, size), 1) // per_group
    return jnp.where(a == b, 1.0, 0.0).astype(BF16)


def group_sum(rows, member):
    hi = rows.astype(BF16).astype(F32)
    rest = rows - hi
    mid = rest.astype(BF16).astype(F32)
    low = rest - mid
    count = rows.shape[0]
    terms = jnp.concatenate([hi, mid, low], axis=0).astype(BF16)
    out = jnp.dot(terms, member, preferred_element_type=F32)
    return out[:count] + out[count : 2 * count] + out[2 * count :]


def block_stats(blocks, member, entries):
    sums = jnp.concatenate([jnp.sum(b, axis=0, keepdims=True) for b in blocks], axis=0)
    means = group_sum(sums, member) / entries
    squares = []
    for n, b in enumerate(blocks):
        d = b - means[n : n + 1]
        squares.append(jnp.sum(d * d, axis=0, keepdims=True))
    return means, group_sum(jnp.concatenate(squares, axis=0), member)


def merge_stats(means, squares, entries):
    count = len(means)
    mean = functools.reduce(lambda a, b: a + b, means) / count
    total = functools.reduce(lambda a, b: a + b, squares)
    for m in means:
        d = m - mean
        total = total + entries * (d * d)
    return mean, lax.rsqrt(total / (count * entries) + EPS)


def kernel(T, R, W, rows, C, OUT,
           feat, g1, s1, w1h, b1, g2, s2, w2h, b2, g3, s3, wqh, wkh, wvh, woh,
           out,
           xin, y1, cols, w1, w2, aw, st1, st2, hs, hfull, normed,
           lsem, blk_s, blk_r, top_s, top_r, bot_s, bot_r, st_s, st_r, hid_s, hid_r):
    t = lax.axis_index("tm")
    z = lax.axis_index("rows")
    me = t * R + z
    N = T * R
    RP = rows * W
    EXT = (rows + 2) * W
    per = C // GROUPS
    entries = RP * per

    loads = [
        pltpu.make_async_copy(w1h, w1.at[:, pl.ds(0, OUT), :], lsem.at[0]),
        pltpu.make_async_copy(w2h, w2.at[:, pl.ds(0, OUT), :], lsem.at[1]),
    ] + [
        pltpu.make_async_copy(src, aw.at[n], lsem.at[2 + n])
        for n, src in enumerate((wqh, wkh, wvh, woh))
    ]
    for load in loads:
        load.start()

    def peer(p):
        other = lax.rem(me + p, N)
        return other // R, lax.rem(other, R)

    barrier = pltpu.get_barrier_semaphore()

    def greet(n):
        pt, pz = peer(n + 1)
        pl.semaphore_signal(barrier, inc=1, device_id={"tm": pt, "rows": pz}, device_id_type=MESH)

    each(N - 1, greet)

    def remote(src, dst, ssem, rsem, pt, pz):
        return pltpu.make_async_remote_copy(
            src_ref=src, dst_ref=dst, send_sem=ssem, recv_sem=rsem,
            device_id={"tm": pt, "rows": pz}, device_id_type=MESH)

    x = feat[...].astype(F32)
    member = membership(C, per)
    mean, square = block_stats([x], member, entries)
    st1[me] = jnp.concatenate([mean, square], axis=0)
    if OUT < LANES:
        w1[:, OUT:, :] = jnp.zeros((27, LANES - OUT, C), BF16)
        w2[:, OUT:, :] = jnp.zeros((27, LANES - OUT, C), BF16)

    pl.semaphore_wait(barrier, N - 1)

    def stat_copy(phase, ref, n):
        pt, pz = peer(n + 1)
        return remote(ref.at[me], ref.at[me], st_s.at[phase, n], st_r.at[phase, me], pt, pz)

    def stat_arrival(phase, ref, n):
        pt, pz = peer(n + 1)
        src = pt * R + pz
        return remote(ref.at[src], ref.at[src], st_s.at[phase, n], st_r.at[phase, src], pt, pz)

    def gather_start(phase, body, first, last, at):
        def send_block(n):
            pt = lax.rem(t + n + 1, T)
            remote(body, at(t, W, RP), blk_s.at[phase, n], blk_r.at[phase, t], pt, z).start()

        def send_down(n):
            pt = lax.rem(t + n, T)
            remote(last, at(t, 0, W), top_s.at[phase, n], top_r.at[phase, t], pt, z + 1).start()

        def send_up(n):
            pt = lax.rem(t + n, T)
            remote(first, at(t, W + RP, W), bot_s.at[phase, n], bot_r.at[phase, t], pt, z - 1).start()

        each(T - 1, send_block)

        @pl.when(z + 1 < R)
        def _():
            each(T, send_down)

        @pl.when(z > 0)
        def _():
            each(T, send_up)

    def gather_sent(phase, body, first, last, at):
        each(T - 1, lambda n: remote(
            body, at(t, W, RP), blk_s.at[phase, n], blk_r.at[phase, t],
            lax.rem(t + n + 1, T), z).wait_send())

        @pl.when(z + 1 < R)
        def _():
            each(T, lambda n: remote(
                last, at(t, 0, W), top_s.at[phase, n], top_r.at[phase, t],
                lax.rem(t + n, T), z + 1).wait_send())

        @pl.when(z > 0)
        def _():
            each(T, lambda n: remote(
                first, at(t, W + RP, W), bot_s.at[phase, n], bot_r.at[phase, t],
                lax.rem(t + n, T), z - 1).wait_send())

    def block_wait(phase, at, n):
        src = lax.rem(t + n, T)
        remote(at(src, W, RP), at(src, W, RP), blk_s.at[phase, 0], blk_r.at[phase, src], src, z).wait_recv()

    def top_wait(phase, at, n):
        src = lax.rem(t + n, T)
        remote(at(src, 0, W), at(src, 0, W), top_s.at[phase, 0], top_r.at[phase, src], src, z - 1).wait_recv()

    def bot_wait(phase, at, n):
        src = lax.rem(t + n, T)
        remote(at(src, W + RP, W), at(src, W + RP, W), bot_s.at[phase, 0], bot_r.at[phase, src], src, z + 1).wait_recv()

    def put_columns(f, offset, value):
        count = value.shape[0]
        active = value * (0.5 * jnp.tanh(0.5 * value) + 0.5)
        col = lax.rem(lax.broadcasted_iota(jnp.int32, (count, C), 0), W)
        before = jnp.where(col == 0, 0.0, pltpu.roll(active, 1, 0))
        after = jnp.where(col == W - 1, 0.0, pltpu.roll(active, count - 1, 0))
        cols[f, pl.ds(offset, count), 0:C] = before.astype(BF16)
        cols[f, pl.ds(offset, count), C : 2 * C] = active.astype(BF16)
        cols[f, pl.ds(offset, count), 2 * C : 3 * C] = after.astype(BF16)

    def conv(weights):
        parts = {}
        for i in range(3):
            frames = T - (2 - i)
            if frames <= 0:
                continue
            total = None
            for j in range(3):
                for k in range(3):
                    window = cols[0:frames, j * W : j * W + RP, k * C : (k + 1) * C]
                    term = lax.dot_general(
                        window.reshape(frames * RP, C), weights[(i * 3 + j) * 3 + k], NT,
                        preferred_element_type=F32)
                    total = term if total is None else total + term
            parts[i] = total
        results = []
        for f in range(T):
            value = parts[2][f * RP : (f + 1) * RP]
            for i in (0, 1):
                src = f + i - 2
                if src >= 0:
                    value = value + parts[i][src * RP : (src + 1) * RP]
            results.append(value)
        return results

    zero_row = jnp.zeros((W, 3 * C), BF16)

    at1 = lambda src, offset, count: xin.at[src, pl.ds(offset, count), :]
    phase1 = (0, feat, feat.at[pl.ds(0, W), :], feat.at[pl.ds(RP - W, W), :], at1)
    each(N - 1, lambda n: stat_copy(0, st1, n).start())
    gather_start(*phase1)
    xin[t, W : W + RP, :] = feat[...]
    each(N - 1, lambda n: stat_arrival(0, st1, n).wait_recv())

    gain1, shift1 = g1[...], s1[...]

    def norm1(f):
        means = [st1[f * R + r, 0:1, :] for r in range(R)]
        squares = [st1[f * R + r, 1:2, :] for r in range(R)]
        mean, inv = merge_stats(means, squares, entries)
        return mean, inv * gain1

    def fill1(f, offset, count):
        mean, scale = norm1(f)
        value = (xin[f, pl.ds(offset, count), :].astype(F32) - mean) * scale + shift1
        put_columns(f, offset, value)

    def body1(n):
        if n > 0:
            block_wait(0, at1, n)
        fill1(lax.rem(t + n, T), W, RP)

    for n in range(T):
        body1(n)

    @pl.when(z > 0)
    def _():
        for n in range(T):
            top_wait(0, at1, n)
            fill1(lax.rem(t + n, T), 0, W)

    @pl.when(z == 0)
    def _():
        for f in range(T):
            cols[f, 0:W, :] = zero_row

    @pl.when(z + 1 < R)
    def _():
        for n in range(T):
            bot_wait(0, at1, n)
            fill1(lax.rem(t + n, T), W + RP, W)

    @pl.when(z + 1 == R)
    def _():
        for f in range(T):
            cols[f, W + RP : EXT, :] = zero_row

    loads[0].wait()
    bias1 = b1[...]
    outs = [(v + bias1).astype(BF16) for v in conv(w1)]
    member_out = membership(LANES, per)
    for f in range(T):
        y1[t, f, W : W + RP, :] = outs[f]
    mean, square = block_stats([v.astype(F32) for v in outs], member_out, entries)
    st2[me, 0] = mean
    st2[me, 1] = square

    at2 = lambda src, offset, count: y1.at[src, :, pl.ds(offset, count), :]
    phase2 = (1, at2(t, W, RP), at2(t, W, W), at2(t, RP, W), at2)
    each(N - 1, lambda n: stat_copy(1, st2, n).start())
    gather_start(*phase2)

    pick = jnp.where(
        (lax.broadcasted_iota(jnp.int32, (C, LANES), 0)
         == t * OUT + lax.broadcasted_iota(jnp.int32, (C, LANES), 1))
        & (lax.broadcasted_iota(jnp.int32, (C, LANES), 1) < OUT), 1.0, 0.0).astype(BF16)
    own = jnp.dot(xin[:, W : W + RP, :].reshape(T * RP, C), pick, preferred_element_type=F32)

    each(N - 1, lambda n: stat_arrival(1, st2, n).wait_recv())
    gain2, shift2 = g2[...], s2[...]
    mean_cols, inv_cols = [], []
    for s in range(T):
        mean, inv = merge_stats(
            [st2[s * R + r, 0] for r in range(R)], [st2[s * R + r, 1] for r in range(R)], entries)
        mean_cols.append(mean[:, :OUT])
        inv_cols.append(inv[:, :OUT])
    mean2 = jnp.concatenate(mean_cols, axis=1)
    scale2 = jnp.concatenate(inv_cols, axis=1) * gain2

    def joined(blocks):
        return jnp.concatenate([b.astype(F32)[:, :OUT] for b in blocks], axis=1)

    def fill2(f, offset, count):
        raw = joined([y1[s, f, offset : offset + count, :] for s in range(T)])
        value = (raw - mean2[f : f + 1]) * scale2[f : f + 1] + shift2
        put_columns(f, offset, value)

    for n in range(1, T):
        block_wait(1, at2, n)
    for f in range(T):
        fill2(f, W, RP)

    @pl.when(z > 0)
    def _():
        for n in range(T):
            top_wait(1, at2, n)
        for f in range(T):
            fill2(f, 0, W)

    @pl.when(z + 1 < R)
    def _():
        for n in range(T):
            bot_wait(1, at2, n)
        for f in range(T):
            fill2(f, W + RP, W)

    loads[1].wait()
    bias2 = b2[...]
    for f, v in enumerate(conv(w2)):
        rounded = (v + bias2).astype(BF16).astype(F32)
        hs[f] = (own[f * RP : (f + 1) * RP] + rounded).astype(BF16)

    def hidden_copy(n):
        pt, pz = peer(n + 1)
        return remote(hs.at[pt], hfull.at[t, pl.ds(z * RP, RP), :], hid_s.at[n], hid_r.at[me], pt, pz)

    def hidden_arrival(n):
        pt, pz = peer(n + 1)
        dst = hfull.at[pt, pl.ds(pz * RP, RP), :]
        return remote(dst, dst, hid_s.at[n], hid_r.at[pt * R + pz], pt, pz)

    each(N - 1, lambda n: hidden_copy(n).start())
    hfull[t, pl.ds(z * RP, RP), :] = hs[t]

    each(N - 1, lambda n: stat_copy(0, st1, n).wait_send())
    gather_sent(*phase1)
    each(N - 1, lambda n: stat_copy(1, st2, n).wait_send())
    gather_sent(*phase2)
    for n in range(2, 6):
        loads[n].wait()

    each(N - 1, lambda n: hidden_arrival(n).wait_recv())

    total_rows = R * RP
    chunk = min(total_rows, 4 * RP)
    parts = total_rows // chunk

    def frame_rows(n):
        start = pl.multiple_of(n * chunk, 16)
        return joined([hfull[s, pl.ds(start, chunk), :] for s in range(T)])

    def fold(body, init):
        if parts == 1:
            return body(0, init)
        return lax.fori_loop(0, parts, body, init)

    zero = jnp.zeros((1, C), F32)
    sums = fold(lambda n, a: a + jnp.sum(frame_rows(n), axis=0, keepdims=True), zero)
    mean = group_sum(sums, member) / (entries * R)

    def deviation(n, a):
        d = frame_rows(n) - mean
        return a + jnp.sum(d * d, axis=0, keepdims=True)

    var = group_sum(fold(deviation, zero), member) / (entries * R)
    scale3 = lax.rsqrt(var + EPS) * g3[...]
    shift3 = s3[...]

    def normalise(n, c):
        start = pl.multiple_of(n * chunk, 16)
        value = ((frame_rows(n) - mean) * scale3 + shift3).astype(BF16)
        normed[0, pl.ds(start, chunk), :] = value
        normed[1, pl.ds(start, chunk), :] = jnp.dot(value, aw[1], preferred_element_type=F32).astype(BF16)
        normed[2, pl.ds(start, chunk), :] = jnp.dot(value, aw[2], preferred_element_type=F32).astype(BF16)
        return c

    fold(normalise, 0)
    mine = pl.ds(pl.multiple_of(z * RP, 16), RP)
    queries = (jnp.dot(normed[0, mine, :], aw[0], preferred_element_type=F32) * C ** (-0.5)).astype(BF16)
    scores = lax.dot_general(queries, normed[1], NT, preferred_element_type=F32)
    peak = jnp.max(scores, axis=1, keepdims=True)
    weights = jnp.exp(scores - peak)
    total = jnp.sum(weights, axis=1, keepdims=True)
    summed = jnp.dot(weights.astype(BF16), normed[2], preferred_element_type=F32)
    attended = (summed / total).astype(BF16)
    hidden = joined([hfull[s, mine, :] for s in range(T)])
    out[...] = (hidden + jnp.dot(attended, aw[3], preferred_element_type=F32)).astype(BF16)

    each(N - 1, lambda n: hidden_copy(n).wait_send())


def solution(mesh):
    T, R = mesh.shape["tm"], mesh.shape["rows"]

    def per_device(features, g1, s1, k1, b1, g2, s2, k2, b2, g3, s3, wq, wk, wv, wo):
        _, rows, W, C = features.shape
        OUT = k1.shape[0]
        RP, EXT, N = rows * W, (rows + 2) * W, T * R
        vec = lambda a: a.reshape(1, -1)
        pad = lambda a: jnp.pad(a, (0, LANES - OUT)).reshape(1, LANES)
        taps = lambda k: jnp.transpose(k, (1, 2, 3, 0, 4)).reshape(27, OUT, C)
        vmem = pl.BlockSpec(memory_space=pltpu.VMEM)
        hbm = pl.BlockSpec(memory_space=pl.ANY)
        dma = pltpu.SemaphoreType.DMA
        result = pl.pallas_call(
            functools.partial(kernel, T, R, W, rows, C, OUT),
            out_shape=jax.ShapeDtypeStruct((RP, C), BF16),
            in_specs=[vmem, vmem, vmem, hbm, vmem, vmem, vmem, hbm, vmem, vmem, vmem, hbm, hbm, hbm, hbm],
            out_specs=vmem,
            scratch_shapes=[
                pltpu.VMEM((T, EXT, C), BF16),
                pltpu.VMEM((T, T, EXT, LANES), BF16),
                pltpu.VMEM((T, EXT, 3 * C), BF16),
                pltpu.VMEM((27, LANES, C), BF16),
                pltpu.VMEM((27, LANES, C), BF16),
                pltpu.VMEM((4, C, C), BF16),
                pltpu.VMEM((N, 2, C), F32),
                pltpu.VMEM((N, 2, T, LANES), F32),
                pltpu.VMEM((T, RP, LANES), BF16),
                pltpu.VMEM((T, R * RP, LANES), BF16),
                pltpu.VMEM((3, R * RP, C), BF16),
                dma((6,)),
                dma((2, T)), dma((2, T)),
                dma((2, T)), dma((2, T)),
                dma((2, T)), dma((2, T)),
                dma((2, N)), dma((2, N)),
                dma((N,)), dma((N,)),
            ],
            compiler_params=pltpu.CompilerParams(
                collective_id=0, has_side_effects=True, vmem_limit_bytes=48 * 1024 * 1024),
        )(features.reshape(RP, C), vec(g1), vec(s1), taps(k1), pad(b1), vec(g2), vec(s2),
          taps(k2), pad(b2), vec(g3), vec(s3), wq, wk, wv, wo)
        return result.reshape(features.shape)

    in_specs = (
        P(("clips", "tm"), "rows", None, None), P(), P(),
        P("tm", None, None, None, None), P("tm"), P(), P(),
        P("tm", None, None, None, None), P("tm"), P(), P(), P(), P(), P(), P(),
    )
    return jax.shard_map(
        per_device, mesh=mesh, in_specs=in_specs,
        out_specs=P(("clips", "tm"), "rows", None, None), check_vma=False)
```

```python
import functools

import jax
import jax.numpy as jnp
from jax import lax
from jax.experimental import pallas as pl
from jax.experimental.pallas import tpu as pltpu
from jax.sharding import PartitionSpec as P

GROUPS = 32
EPS = 1e-06
LANES = 128
MESH = pl.DeviceIdType.MESH
F32 = jnp.float32
BF16 = jnp.bfloat16
NT = (((1,), (1,)), ((), ()))


def flat(ref):
    return ref[...].reshape(1, ref.shape[0])


def padded(ref):
    row = flat(ref)
    rest = LANES - ref.shape[0]
    return jnp.concatenate([row, jnp.zeros((1, rest), F32)], axis=1) if rest else row


def each(count, body):
    if count <= 16:
        for n in range(count):
            body(n)
    else:
        lax.fori_loop(0, count, lambda n, c: (body(n), c)[1], 0)


def membership(size, per_group):
    a = lax.broadcasted_iota(jnp.int32, (size, size), 0) // per_group
    b = lax.broadcasted_iota(jnp.int32, (size, size), 1) // per_group
    return jnp.where(a == b, 1.0, 0.0).astype(BF16)


def group_sum(rows, member):
    hi = rows.astype(BF16).astype(F32)
    rest = rows - hi
    mid = rest.astype(BF16).astype(F32)
    low = rest - mid
    count = rows.shape[0]
    terms = jnp.concatenate([hi, mid, low], axis=0).astype(BF16)
    out = jnp.dot(terms, member, preferred_element_type=F32)
    return out[:count] + out[count : 2 * count] + out[2 * count :]


def block_stats(blocks, member, entries):
    sums = jnp.concatenate([jnp.sum(b, axis=0, keepdims=True) for b in blocks], axis=0)
    means = group_sum(sums, member) / entries
    squares = []
    for n, b in enumerate(blocks):
        d = b - means[n : n + 1]
        squares.append(jnp.sum(d * d, axis=0, keepdims=True))
    return means, group_sum(jnp.concatenate(squares, axis=0), member)


def merge_stats(means, squares, entries):
    count = len(means)
    mean = functools.reduce(lambda a, b: a + b, means) / count
    total = functools.reduce(lambda a, b: a + b, squares)
    for m in means:
        d = m - mean
        total = total + entries * (d * d)
    return mean, lax.rsqrt(total / (count * entries) + EPS)


def kernel(T, R, W, rows, C, OUT,
           feath, g1h, s1h, w1h, b1h, g2h, s2h, w2h, b2h, g3h, s3h, wqh, wkh, wvh, woh,
           out,
           feat, g1, s1, g2, s2, g3, s3, b1, b2, xin, y1, cols, w1, w2, aw, st1, st2, hs, hfull, normed,
           lsem, blk_s, blk_r, top_s, top_r, bot_s, bot_r, st_s, st_r, hid_s, hid_r):
    t = lax.axis_index("tm")
    z = lax.axis_index("rows")
    me = t * R + z
    N = T * R
    RP = rows * W
    EXT = (rows + 2) * W
    per = C // GROUPS
    entries = RP * per

    loads = [
        pltpu.make_async_copy(w1h, w1.at[:, pl.ds(0, OUT), :], lsem.at[0]),
        pltpu.make_async_copy(w2h, w2.at[:, pl.ds(0, OUT), :], lsem.at[1]),
    ] + [
        pltpu.make_async_copy(src, aw.at[n], lsem.at[2 + n])
        for n, src in enumerate((wqh, wkh, wvh, woh))
    ]
    small = [
        pltpu.make_async_copy(src, dst, lsem.at[6 + n])
        for n, (src, dst) in enumerate((
            (feath, feat), (g1h, g1), (s1h, s1), (g2h, g2), (s2h, s2), (g3h, g3), (s3h, s3),
            (b1h, b1), (b2h, b2)))
    ]
    for load in small + loads:
        load.start()

    def peer(p):
        other = lax.rem(me + p, N)
        return other // R, lax.rem(other, R)

    barrier = pltpu.get_barrier_semaphore()

    def greet(n):
        pt, pz = peer(n + 1)
        pl.semaphore_signal(barrier, inc=1, device_id={"tm": pt, "rows": pz}, device_id_type=MESH)

    each(N - 1, greet)

    def remote(src, dst, ssem, rsem, pt, pz):
        return pltpu.make_async_remote_copy(
            src_ref=src, dst_ref=dst, send_sem=ssem, recv_sem=rsem,
            device_id={"tm": pt, "rows": pz}, device_id_type=MESH)

    for load in small:
        load.wait()
    x = feat[...].astype(F32)
    member = membership(C, per)
    mean, square = block_stats([x], member, entries)
    st1[me] = jnp.concatenate([mean, square], axis=0)
    if OUT < LANES:
        w1[:, OUT:, :] = jnp.zeros((27, LANES - OUT, C), BF16)
        w2[:, OUT:, :] = jnp.zeros((27, LANES - OUT, C), BF16)

    pl.semaphore_wait(barrier, N - 1)

    def stat_copy(phase, ref, n):
        pt, pz = peer(n + 1)
        return remote(ref.at[me], ref.at[me], st_s.at[phase, n], st_r.at[phase, me], pt, pz)

    def stat_arrival(phase, ref, n):
        pt, pz = peer(n + 1)
        src = pt * R + pz
        return remote(ref.at[src], ref.at[src], st_s.at[phase, n], st_r.at[phase, src], pt, pz)

    core = lax.rem(t, 2)
    sib = t + 1 - 2 * core
    X = T // 2
    chip = t // 2

    def same(n):
        return 2 * lax.rem(chip + n, X) + core

    def other(n):
        return 2 * lax.rem(chip + n, X) + 1 - core

    def pieces(phase, body, first, last, at):
        blocks = [remote(body, at(t, W, RP), blk_s.at[phase, n], blk_r.at[phase, t], same(n), z)
                  for n in range(1, X)]
        blocks.append(remote(body, at(t, W, RP), blk_s.at[phase, 0], blk_r.at[phase, t], sib, z))
        down = [remote(last, at(t, 0, W), top_s.at[phase, n], top_r.at[phase, t], same(n), z + 1)
                for n in range(X)]
        up = [remote(first, at(t, W + RP, W), bot_s.at[phase, n], bot_r.at[phase, t], same(n), z - 1)
              for n in range(X)]
        return blocks, down, up

    def gather_start(*args):
        blocks, down, up = pieces(*args)
        for c in blocks:
            c.start()

        @pl.when(z + 1 < R)
        def _():
            for c in down[1:] + down[:1]:
                c.start()

        @pl.when(z > 0)
        def _():
            for c in up[1:] + up[:1]:
                c.start()

    def forward(phase, at, sems, offset, count, src, n):
        ssem, rsem = sems
        return remote(at(src, offset, count), at(src, offset, count),
                      ssem.at[phase, X + n], rsem.at[phase, src], sib, z)

    blk, top, bot = (blk_s, blk_r), (top_s, top_r), (bot_s, bot_r)
    forwards = ((blk, W, RP, 1), (top, 0, W, 0), (bot, W + RP, W, 0))

    def relay(phase, at, which):
        sems, offset, count, start = forwards[which]
        for n in range(start, X):
            c = forward(phase, at, sems, offset, count, same(n), n)
            c.wait_recv()
            c.start()

    def sibling_wait(phase, at, which):
        sems, offset, count, _ = forwards[which]
        for n in range(X):
            forward(phase, at, sems, offset, count, other(n), n).wait_recv()

    def gather_sent(*args):
        phase, at = args[0], args[4]
        blocks, down, up = pieces(*args)
        for c in blocks:
            c.wait_send()
        for n in range(1, X):
            forward(phase, at, blk, W, RP, same(n), n).wait_send()

        @pl.when(z + 1 < R)
        def _():
            for c in down:
                c.wait_send()
            for n in range(X):
                forward(phase, at, bot, W + RP, W, same(n), n).wait_send()

        @pl.when(z > 0)
        def _():
            for c in up:
                c.wait_send()
            for n in range(X):
                forward(phase, at, top, 0, W, same(n), n).wait_send()

    def put_columns(f, offset, value):
        count = value.shape[0]
        active = value * (0.5 * jnp.tanh(0.5 * value) + 0.5)
        col = lax.rem(lax.broadcasted_iota(jnp.int32, (count, C), 0), W)
        before = jnp.where(col == 0, 0.0, pltpu.roll(active, 1, 0))
        after = jnp.where(col == W - 1, 0.0, pltpu.roll(active, count - 1, 0))
        cols[f, pl.ds(offset, count), 0:C] = before.astype(BF16)
        cols[f, pl.ds(offset, count), C : 2 * C] = active.astype(BF16)
        cols[f, pl.ds(offset, count), 2 * C : 3 * C] = after.astype(BF16)

    def conv(weights):
        parts = {}
        for i in range(3):
            frames = T - (2 - i)
            if frames <= 0:
                continue
            total = None
            for j in range(3):
                for k in range(3):
                    window = cols[0:frames, j * W : j * W + RP, k * C : (k + 1) * C]
                    term = lax.dot_general(
                        window.reshape(frames * RP, C), weights[(i * 3 + j) * 3 + k], NT,
                        preferred_element_type=F32)
                    total = term if total is None else total + term
            parts[i] = total
        results = []
        for f in range(T):
            value = parts[2][f * RP : (f + 1) * RP]
            for i in (0, 1):
                src = f + i - 2
                if src >= 0:
                    value = value + parts[i][src * RP : (src + 1) * RP]
            results.append(value)
        return results

    zero_row = jnp.zeros((W, 3 * C), BF16)

    at1 = lambda src, offset, count: xin.at[src, pl.ds(offset, count), :]
    phase1 = (0, feat, feat.at[pl.ds(0, W), :], feat.at[pl.ds(RP - W, W), :], at1)
    each(N - 1, lambda n: stat_copy(0, st1, n).start())
    gather_start(*phase1)
    xin[t, W : W + RP, :] = feat[...]
    each(N - 1, lambda n: stat_arrival(0, st1, n).wait_recv())

    gain1, shift1 = flat(g1), flat(s1)

    def norm1(f):
        means = [st1[f * R + r, 0:1, :] for r in range(R)]
        squares = [st1[f * R + r, 1:2, :] for r in range(R)]
        mean, inv = merge_stats(means, squares, entries)
        return mean, inv * gain1

    def fill1(f, offset, count):
        mean, scale = norm1(f)
        value = (xin[f, pl.ds(offset, count), :].astype(F32) - mean) * scale + shift1
        put_columns(f, offset, value)

    fill1(t, W, RP)
    relay(0, at1, 0)

    @pl.when(z > 0)
    def _():
        relay(0, at1, 1)

    @pl.when(z + 1 < R)
    def _():
        relay(0, at1, 2)

    for n in range(1, X):
        fill1(same(n), W, RP)
    sibling_wait(0, at1, 0)
    for n in range(X):
        fill1(other(n), W, RP)

    @pl.when(z > 0)
    def _():
        sibling_wait(0, at1, 1)
        for f in range(T):
            fill1(f, 0, W)

    @pl.when(z == 0)
    def _():
        for f in range(T):
            cols[f, 0:W, :] = zero_row

    @pl.when(z + 1 < R)
    def _():
        sibling_wait(0, at1, 2)
        for f in range(T):
            fill1(f, W + RP, W)

    @pl.when(z + 1 == R)
    def _():
        for f in range(T):
            cols[f, W + RP : EXT, :] = zero_row

    loads[0].wait()
    bias1 = padded(b1)
    outs = [(v + bias1).astype(BF16) for v in conv(w1)]
    member_out = membership(LANES, per)
    for f in range(T):
        y1[t, f, W : W + RP, :] = outs[f]
    mean, square = block_stats([v.astype(F32) for v in outs], member_out, entries)
    st2[me, 0] = mean
    st2[me, 1] = square

    at2 = lambda src, offset, count: y1.at[src, :, pl.ds(offset, count), :]
    phase2 = (1, at2(t, W, RP), at2(t, W, W), at2(t, RP, W), at2)
    each(N - 1, lambda n: stat_copy(1, st2, n).start())
    gather_start(*phase2)

    pick = jnp.where(
        (lax.broadcasted_iota(jnp.int32, (C, LANES), 0)
         == t * OUT + lax.broadcasted_iota(jnp.int32, (C, LANES), 1))
        & (lax.broadcasted_iota(jnp.int32, (C, LANES), 1) < OUT), 1.0, 0.0).astype(BF16)
    own = jnp.dot(xin[:, W : W + RP, :].reshape(T * RP, C), pick, preferred_element_type=F32)

    each(N - 1, lambda n: stat_arrival(1, st2, n).wait_recv())
    gain2, shift2 = flat(g2), flat(s2)
    mean_cols, inv_cols = [], []
    for s in range(T):
        mean, inv = merge_stats(
            [st2[s * R + r, 0] for r in range(R)], [st2[s * R + r, 1] for r in range(R)], entries)
        mean_cols.append(mean[:, :OUT])
        inv_cols.append(inv[:, :OUT])
    mean2 = jnp.concatenate(mean_cols, axis=1)
    scale2 = jnp.concatenate(inv_cols, axis=1) * gain2

    def joined(blocks):
        return jnp.concatenate([b.astype(F32)[:, :OUT] for b in blocks], axis=1)

    def fill2(f, offset, count):
        raw = joined([y1[s, f, offset : offset + count, :] for s in range(T)])
        value = (raw - mean2[f : f + 1]) * scale2[f : f + 1] + shift2
        put_columns(f, offset, value)

    relay(1, at2, 0)

    @pl.when(z > 0)
    def _():
        relay(1, at2, 1)

    @pl.when(z + 1 < R)
    def _():
        relay(1, at2, 2)

    sibling_wait(1, at2, 0)
    for f in range(T):
        fill2(f, W, RP)

    @pl.when(z > 0)
    def _():
        sibling_wait(1, at2, 1)
        for f in range(T):
            fill2(f, 0, W)

    @pl.when(z + 1 < R)
    def _():
        sibling_wait(1, at2, 2)
        for f in range(T):
            fill2(f, W + RP, W)

    loads[1].wait()
    bias2 = padded(b2)
    for f, v in enumerate(conv(w2)):
        rounded = (v + bias2).astype(BF16).astype(F32)
        hs[f] = (own[f * RP : (f + 1) * RP] + rounded).astype(BF16)

    def place(src, zz):
        return hfull.at[src, pl.ds(pl.multiple_of(zz * RP, 16), RP), :]

    def hidden_copy(n):
        pt = lax.rem(t + n + 1, T)
        return remote(hs.at[pt], place(t, z), hid_s.at[2, n], hid_r.at[me], pt, z)

    def passed(way, src, zz):
        return remote(place(src, zz), place(src, zz), hid_s.at[way, src * R + zz],
                      hid_r.at[src * R + zz], t, z + 1 if way == 0 else z - 1)

    def along(act, begin):
        def step(m):
            d = m + begin

            @pl.when(z - d >= 0)
            def _():
                for n in range(T):
                    act(lax.rem(t + n, T), z - d, 0)

            @pl.when(z + d < R)
            def _():
                for n in range(T):
                    act(lax.rem(t + n, T), z + d, 1)

        each(R - begin, step)

    each(T - 1, lambda n: hidden_copy(n).start())
    hfull[t, pl.ds(pl.multiple_of(z * RP, 16), RP), :] = hs[t]

    def onward(src, zz, way):
        @pl.when(z + 1 < R if way == 0 else z > 0)
        def _():
            passed(way, src, zz).start()

    for n in range(T):
        src = lax.rem(t + n, T)
        if n > 0:
            passed(0, src, z).wait_recv()
        onward(src, z, 0)
        onward(src, z, 1)

    def arrive(src, zz, way):
        passed(way, src, zz).wait_recv()
        onward(src, zz, way)

    along(arrive, 1)

    each(N - 1, lambda n: stat_copy(0, st1, n).wait_send())
    gather_sent(*phase1)
    each(N - 1, lambda n: stat_copy(1, st2, n).wait_send())
    gather_sent(*phase2)
    for n in range(2, 6):
        loads[n].wait()

    total_rows = R * RP
    chunk = min(total_rows, 4 * RP)
    parts = total_rows // chunk

    def frame_rows(n):
        start = pl.multiple_of(n * chunk, 16)
        return joined([hfull[s, pl.ds(start, chunk), :] for s in range(T)])

    def fold(body, init):
        if parts == 1:
            return body(0, init)
        return lax.fori_loop(0, parts, body, init)

    zero = jnp.zeros((1, C), F32)
    sums = fold(lambda n, a: a + jnp.sum(frame_rows(n), axis=0, keepdims=True), zero)
    mean = group_sum(sums, member) / (entries * R)

    def deviation(n, a):
        d = frame_rows(n) - mean
        return a + jnp.sum(d * d, axis=0, keepdims=True)

    var = group_sum(fold(deviation, zero), member) / (entries * R)
    scale3 = lax.rsqrt(var + EPS) * flat(g3)
    shift3 = flat(s3)

    def normalise(n, c):
        start = pl.multiple_of(n * chunk, 16)
        value = ((frame_rows(n) - mean) * scale3 + shift3).astype(BF16)
        normed[0, pl.ds(start, chunk), :] = value
        normed[1, pl.ds(start, chunk), :] = jnp.dot(value, aw[1], preferred_element_type=F32).astype(BF16)
        normed[2, pl.ds(start, chunk), :] = jnp.dot(value, aw[2], preferred_element_type=F32).astype(BF16)
        return c

    fold(normalise, 0)
    mine = pl.ds(pl.multiple_of(z * RP, 16), RP)
    queries = (jnp.dot(normed[0, mine, :], aw[0], preferred_element_type=F32) * C ** (-0.5)).astype(BF16)
    scores = lax.dot_general(queries, normed[1], NT, preferred_element_type=F32)
    peak = jnp.max(scores, axis=1, keepdims=True)
    weights = jnp.exp(scores - peak)
    total = jnp.sum(weights, axis=1, keepdims=True)
    summed = jnp.dot(weights.astype(BF16), normed[2], preferred_element_type=F32)
    attended = (summed / total).astype(BF16)
    hidden = joined([hfull[s, mine, :] for s in range(T)])
    out[...] = (hidden + jnp.dot(attended, aw[3], preferred_element_type=F32)).astype(BF16)

    each(T - 1, lambda n: hidden_copy(n).wait_send())

    def left(src, zz, way):
        @pl.when(z + 1 < R if way == 0 else z > 0)
        def _():
            passed(way, src, zz).wait_send()

    for n in range(T):
        left(lax.rem(t + n, T), z, 0)
        left(lax.rem(t + n, T), z, 1)
    along(left, 1)


def solution(mesh):
    T, R = mesh.shape["tm"], mesh.shape["rows"]

    def per_device(features, g1, s1, k1, b1, g2, s2, k2, b2, g3, s3, wq, wk, wv, wo):
        _, rows, W, C = features.shape
        OUT = k1.shape[0]
        RP, EXT, N = rows * W, (rows + 2) * W, T * R
        taps = lambda k: jnp.transpose(k, (1, 2, 3, 0, 4)).reshape(27, OUT, C)
        vmem = pl.BlockSpec(memory_space=pltpu.VMEM)
        hbm = pl.BlockSpec(memory_space=pltpu.HBM)
        dma = pltpu.SemaphoreType.DMA
        result = pl.pallas_call(
            functools.partial(kernel, T, R, W, rows, C, OUT),
            out_shape=jax.ShapeDtypeStruct((RP, C), BF16),
            in_specs=[hbm] * 15,
            out_specs=vmem,
            scratch_shapes=[pltpu.VMEM((RP, C), BF16)] + [pltpu.VMEM((C,), F32)] * 6
            + [pltpu.VMEM((OUT,), F32)] * 2 + [
                pltpu.VMEM((T, EXT, C), BF16),
                pltpu.VMEM((T, T, EXT, LANES), BF16),
                pltpu.VMEM((T, EXT, 3 * C), BF16),
                pltpu.VMEM((27, LANES, C), BF16),
                pltpu.VMEM((27, LANES, C), BF16),
                pltpu.VMEM((4, C, C), BF16),
                pltpu.VMEM((N, 2, C), F32),
                pltpu.VMEM((N, 2, T, LANES), F32),
                pltpu.VMEM((T, RP, LANES), BF16),
                pltpu.VMEM((T, R * RP, LANES), BF16),
                pltpu.VMEM((3, R * RP, C), BF16),
                dma((15,)),
                dma((2, T)), dma((2, T)),
                dma((2, T)), dma((2, T)),
                dma((2, T)), dma((2, T)),
                dma((2, N)), dma((2, N)),
                dma((3, N)), dma((N,)),
            ],
            compiler_params=pltpu.CompilerParams(
                collective_id=0, has_side_effects=True, vmem_limit_bytes=62 * 1024 * 1024),
        )(features.reshape(RP, C), g1, s1, taps(k1), b1, g2, s2,
          taps(k2), b2, g3, s3, wq, wk, wv, wo)
        return result.reshape(features.shape)

    in_specs = (
        P(("clips", "tm"), "rows", None, None), P(), P(),
        P("tm", None, None, None, None), P("tm"), P(), P(),
        P("tm", None, None, None, None), P("tm"), P(), P(), P(), P(), P(), P(),
    )
    return jax.shard_map(
        per_device, mesh=mesh, in_specs=in_specs,
        out_specs=P(("clips", "tm"), "rows", None, None), check_vma=False)
```

```python
import functools

import jax
import jax.numpy as jnp
from jax import lax
from jax.experimental import pallas as pl
from jax.experimental.pallas import tpu as pltpu
from jax.sharding import PartitionSpec as P

GROUPS = 32
EPS = 1e-06
LANES = 128
MESH = pl.DeviceIdType.MESH
F32 = jnp.float32
BF16 = jnp.bfloat16
NT = (((1,), (1,)), ((), ()))


def flat(ref):
    return ref[...].reshape(1, ref.shape[0])


def padded(ref):
    row = flat(ref)
    rest = LANES - ref.shape[0]
    return jnp.concatenate([row, jnp.zeros((1, rest), F32)], axis=1) if rest else row


def each(count, body):
    if count <= 16:
        for n in range(count):
            body(n)
    else:
        lax.fori_loop(0, count, lambda n, c: (body(n), c)[1], 0)


def membership(size, per_group):
    a = lax.broadcasted_iota(jnp.int32, (size, size), 0) // per_group
    b = lax.broadcasted_iota(jnp.int32, (size, size), 1) // per_group
    return jnp.where(a == b, 1.0, 0.0).astype(BF16)


def group_sum(rows, member):
    hi = rows.astype(BF16).astype(F32)
    rest = rows - hi
    mid = rest.astype(BF16).astype(F32)
    low = rest - mid
    count = rows.shape[0]
    terms = jnp.concatenate([hi, mid, low], axis=0).astype(BF16)
    out = jnp.dot(terms, member, preferred_element_type=F32)
    return out[:count] + out[count : 2 * count] + out[2 * count :]


def block_stats(blocks, member, entries):
    sums = jnp.concatenate([jnp.sum(b, axis=0, keepdims=True) for b in blocks], axis=0)
    means = group_sum(sums, member) / entries
    squares = []
    for n, b in enumerate(blocks):
        d = b - means[n : n + 1]
        squares.append(jnp.sum(d * d, axis=0, keepdims=True))
    return means, group_sum(jnp.concatenate(squares, axis=0), member)


def merge_stats(means, squares, entries):
    count = len(means)
    mean = functools.reduce(lambda a, b: a + b, means) / count
    total = functools.reduce(lambda a, b: a + b, squares)
    for m in means:
        d = m - mean
        total = total + entries * (d * d)
    return mean, lax.rsqrt(total / (count * entries) + EPS)


def kernel(T, R, W, rows, C, OUT,
           feath, g1h, s1h, w1h, b1h, g2h, s2h, w2h, b2h, g3h, s3h, wqh, wkh, wvh, woh,
           out,
           feat, g1, s1, g2, s2, g3, s3, b1, b2, xin, y1, cols, w1, w2, aw, st1, st2, hs, hfull, normed,
           lsem, blk_s, blk_r, top_s, top_r, bot_s, bot_r, st_s, st_r, hid_s, hid_r):
    t = lax.axis_index("tm")
    z = lax.axis_index("rows")
    me = t * R + z
    N = T * R
    RP = rows * W
    EXT = (rows + 2) * W
    per = C // GROUPS
    entries = RP * per

    loads = [
        pltpu.make_async_copy(w1h, w1.at[:, pl.ds(0, OUT), :], lsem.at[0]),
        pltpu.make_async_copy(w2h, w2.at[:, pl.ds(0, OUT), :], lsem.at[1]),
    ] + [
        pltpu.make_async_copy(src, aw.at[n], lsem.at[2 + n])
        for n, src in enumerate((wqh, wkh, wvh, woh))
    ]
    small = [
        pltpu.make_async_copy(src, dst, lsem.at[6 + n])
        for n, (src, dst) in enumerate((
            (feath, feat), (g1h, g1), (s1h, s1), (g2h, g2), (s2h, s2), (g3h, g3), (s3h, s3),
            (b1h, b1), (b2h, b2)))
    ]
    for load in small + loads:
        load.start()

    def peer(p):
        other = lax.rem(me + p, N)
        return other // R, lax.rem(other, R)

    barrier = pltpu.get_barrier_semaphore()

    def greet(n):
        pt, pz = peer(n + 1)
        pl.semaphore_signal(barrier, inc=1, device_id={"tm": pt, "rows": pz}, device_id_type=MESH)

    each(N - 1, greet)

    def remote(src, dst, ssem, rsem, pt, pz):
        return pltpu.make_async_remote_copy(
            src_ref=src, dst_ref=dst, send_sem=ssem, recv_sem=rsem,
            device_id={"tm": pt, "rows": pz}, device_id_type=MESH)

    for load in small:
        load.wait()
    x = feat[...].astype(F32)
    member = membership(C, per)
    mean, square = block_stats([x], member, entries)
    st1[me] = jnp.concatenate([mean, square], axis=0)
    if OUT < LANES:
        w1[:, OUT:, :] = jnp.zeros((27, LANES - OUT, C), BF16)
        w2[:, OUT:, :] = jnp.zeros((27, LANES - OUT, C), BF16)

    pl.semaphore_wait(barrier, N - 1)

    def stat_copy(phase, ref, n):
        pt, pz = peer(n + 1)
        return remote(ref.at[me], ref.at[me], st_s.at[phase, n], st_r.at[phase, me], pt, pz)

    def stat_arrival(phase, ref, n):
        pt, pz = peer(n + 1)
        src = pt * R + pz
        return remote(ref.at[src], ref.at[src], st_s.at[phase, n], st_r.at[phase, src], pt, pz)

    core = lax.rem(t, 2)
    sib = t + 1 - 2 * core
    X = T // 2
    chip = t // 2

    def same(n):
        return 2 * lax.rem(chip + n, X) + core

    def other(n):
        return 2 * lax.rem(chip + n, X) + 1 - core

    def pieces(phase, body, first, last, at):
        blocks = [remote(body, at(t, W, RP), blk_s.at[phase, n], blk_r.at[phase, t], same(n), z)
                  for n in range(1, X)]
        blocks.append(remote(body, at(t, W, RP), blk_s.at[phase, 0], blk_r.at[phase, t], sib, z))
        down = [remote(last, at(t, 0, W), top_s.at[phase, n], top_r.at[phase, t], same(n), z + 1)
                for n in range(X)]
        up = [remote(first, at(t, W + RP, W), bot_s.at[phase, n], bot_r.at[phase, t], same(n), z - 1)
              for n in range(X)]
        return blocks, down, up

    def gather_start(*args):
        blocks, down, up = pieces(*args)
        for c in blocks:
            c.start()

        @pl.when(z + 1 < R)
        def _():
            for c in down[1:] + down[:1]:
                c.start()

        @pl.when(z > 0)
        def _():
            for c in up[1:] + up[:1]:
                c.start()

    def forward(phase, at, sems, offset, count, src, n):
        ssem, rsem = sems
        return remote(at(src, offset, count), at(src, offset, count),
                      ssem.at[phase, X + n], rsem.at[phase, src], sib, z)

    blk, top, bot = (blk_s, blk_r), (top_s, top_r), (bot_s, bot_r)
    forwards = ((blk, W, RP, 1), (top, 0, W, 0), (bot, W + RP, W, 0))

    def relay(phase, at, which):
        sems, offset, count, start = forwards[which]
        for n in range(start, X):
            c = forward(phase, at, sems, offset, count, same(n), n)
            c.wait_recv()
            c.start()

    def sibling_wait(phase, at, which):
        sems, offset, count, _ = forwards[which]
        for n in range(X):
            forward(phase, at, sems, offset, count, other(n), n).wait_recv()

    def gather_sent(*args):
        phase, at = args[0], args[4]
        blocks, down, up = pieces(*args)
        for c in blocks:
            c.wait_send()
        for n in range(1, X):
            forward(phase, at, blk, W, RP, same(n), n).wait_send()

        @pl.when(z + 1 < R)
        def _():
            for c in down:
                c.wait_send()
            for n in range(X):
                forward(phase, at, bot, W + RP, W, same(n), n).wait_send()

        @pl.when(z > 0)
        def _():
            for c in up:
                c.wait_send()
            for n in range(X):
                forward(phase, at, top, 0, W, same(n), n).wait_send()

    def put_columns(f, offset, value):
        count = value.shape[0]
        active = value * (0.5 * jnp.tanh(0.5 * value) + 0.5)
        col = lax.rem(lax.broadcasted_iota(jnp.int32, (count, C), 0), W)
        before = jnp.where(col == 0, 0.0, pltpu.roll(active, 1, 0))
        after = jnp.where(col == W - 1, 0.0, pltpu.roll(active, count - 1, 0))
        cols[f, pl.ds(offset, count), 0:C] = before.astype(BF16)
        cols[f, pl.ds(offset, count), C : 2 * C] = active.astype(BF16)
        cols[f, pl.ds(offset, count), 2 * C : 3 * C] = after.astype(BF16)

    def conv(weights):
        parts = {}
        for i in range(3):
            frames = T - (2 - i)
            if frames <= 0:
                continue
            total = None
            for j in range(3):
                for k in range(3):
                    window = cols[0:frames, j * W : j * W + RP, k * C : (k + 1) * C]
                    term = lax.dot_general(
                        window.reshape(frames * RP, C), weights[(i * 3 + j) * 3 + k], NT,
                        preferred_element_type=F32)
                    total = term if total is None else total + term
            parts[i] = total
        results = []
        for f in range(T):
            value = parts[2][f * RP : (f + 1) * RP]
            for i in (0, 1):
                src = f + i - 2
                if src >= 0:
                    value = value + parts[i][src * RP : (src + 1) * RP]
            results.append(value)
        return results

    zero_row = jnp.zeros((W, 3 * C), BF16)

    at1 = lambda src, offset, count: xin.at[src, pl.ds(offset, count), :]
    phase1 = (0, feat, feat.at[pl.ds(0, W), :], feat.at[pl.ds(RP - W, W), :], at1)
    each(N - 1, lambda n: stat_copy(0, st1, n).start())
    gather_start(*phase1)
    xin[t, W : W + RP, :] = feat[...]
    each(N - 1, lambda n: stat_arrival(0, st1, n).wait_recv())

    gain1, shift1 = flat(g1), flat(s1)

    def norm1(f):
        means = [st1[f * R + r, 0:1, :] for r in range(R)]
        squares = [st1[f * R + r, 1:2, :] for r in range(R)]
        mean, inv = merge_stats(means, squares, entries)
        return mean, inv * gain1

    def fill1(f, offset, count):
        mean, scale = norm1(f)
        value = (xin[f, pl.ds(offset, count), :].astype(F32) - mean) * scale + shift1
        put_columns(f, offset, value)

    fill1(t, W, RP)
    relay(0, at1, 0)

    @pl.when(z > 0)
    def _():
        relay(0, at1, 1)

    @pl.when(z + 1 < R)
    def _():
        relay(0, at1, 2)

    for n in range(1, X):
        fill1(same(n), W, RP)
    sibling_wait(0, at1, 0)
    for n in range(X):
        fill1(other(n), W, RP)

    @pl.when(z > 0)
    def _():
        sibling_wait(0, at1, 1)
        for f in range(T):
            fill1(f, 0, W)

    @pl.when(z == 0)
    def _():
        for f in range(T):
            cols[f, 0:W, :] = zero_row

    @pl.when(z + 1 < R)
    def _():
        sibling_wait(0, at1, 2)
        for f in range(T):
            fill1(f, W + RP, W)

    @pl.when(z + 1 == R)
    def _():
        for f in range(T):
            cols[f, W + RP : EXT, :] = zero_row

    loads[0].wait()
    bias1 = padded(b1)
    outs = [(v + bias1).astype(BF16) for v in conv(w1)]
    member_out = membership(LANES, per)
    for f in range(T):
        y1[t, f, W : W + RP, :] = outs[f]
    mean, square = block_stats([v.astype(F32) for v in outs], member_out, entries)
    st2[me, 0] = mean
    st2[me, 1] = square

    at2 = lambda src, offset, count: y1.at[src, :, pl.ds(offset, count), :]
    phase2 = (1, at2(t, W, RP), at2(t, W, W), at2(t, RP, W), at2)
    each(N - 1, lambda n: stat_copy(1, st2, n).start())
    gather_start(*phase2)

    pick = jnp.where(
        (lax.broadcasted_iota(jnp.int32, (C, LANES), 0)
         == t * OUT + lax.broadcasted_iota(jnp.int32, (C, LANES), 1))
        & (lax.broadcasted_iota(jnp.int32, (C, LANES), 1) < OUT), 1.0, 0.0).astype(BF16)
    own = jnp.dot(xin[:, W : W + RP, :].reshape(T * RP, C), pick, preferred_element_type=F32)

    each(N - 1, lambda n: stat_arrival(1, st2, n).wait_recv())
    gain2, shift2 = flat(g2), flat(s2)
    mean_cols, inv_cols = [], []
    for s in range(T):
        mean, inv = merge_stats(
            [st2[s * R + r, 0] for r in range(R)], [st2[s * R + r, 1] for r in range(R)], entries)
        mean_cols.append(mean[:, :OUT])
        inv_cols.append(inv[:, :OUT])
    mean2 = jnp.concatenate(mean_cols, axis=1)
    scale2 = jnp.concatenate(inv_cols, axis=1) * gain2

    def joined(blocks):
        return jnp.concatenate([b.astype(F32)[:, :OUT] for b in blocks], axis=1)

    def fill2(f, offset, count):
        raw = joined([y1[s, f, offset : offset + count, :] for s in range(T)])
        value = (raw - mean2[f : f + 1]) * scale2[f : f + 1] + shift2
        put_columns(f, offset, value)

    relay(1, at2, 0)

    @pl.when(z > 0)
    def _():
        relay(1, at2, 1)

    @pl.when(z + 1 < R)
    def _():
        relay(1, at2, 2)

    sibling_wait(1, at2, 0)
    for f in range(T):
        fill2(f, W, RP)

    @pl.when(z > 0)
    def _():
        sibling_wait(1, at2, 1)
        for f in range(T):
            fill2(f, 0, W)

    @pl.when(z + 1 < R)
    def _():
        sibling_wait(1, at2, 2)
        for f in range(T):
            fill2(f, W + RP, W)

    loads[1].wait()
    bias2 = padded(b2)
    for f, v in enumerate(conv(w2)):
        rounded = (v + bias2).astype(BF16).astype(F32)
        hs[f] = (own[f * RP : (f + 1) * RP] + rounded).astype(BF16)

    def place(src, zz):
        return hfull.at[src, pl.ds(pl.multiple_of(zz * RP, 16), RP), :]

    def hidden_copy(n):
        pt, pz = peer(n + 1)
        return remote(hs.at[pt], place(t, z), hid_s.at[n], hid_r.at[me], pt, pz)

    def hidden_arrival(n):
        pt, pz = peer(n + 1)
        return remote(place(pt, pz), place(pt, pz), hid_s.at[n], hid_r.at[pt * R + pz], pt, pz)

    each(N - 1, lambda n: hidden_copy(n).start())
    hfull[t, pl.ds(pl.multiple_of(z * RP, 16), RP), :] = hs[t]

    each(N - 1, lambda n: stat_copy(0, st1, n).wait_send())
    gather_sent(*phase1)
    each(N - 1, lambda n: stat_copy(1, st2, n).wait_send())
    gather_sent(*phase2)
    for n in range(2, 6):
        loads[n].wait()

    each(N - 1, lambda n: hidden_arrival(n).wait_recv())

    total_rows = R * RP
    chunk = min(total_rows, 4 * RP)
    parts = total_rows // chunk

    def frame_rows(n):
        start = pl.multiple_of(n * chunk, 16)
        return joined([hfull[s, pl.ds(start, chunk), :] for s in range(T)])

    def fold(body, init):
        if parts == 1:
            return body(0, init)
        return lax.fori_loop(0, parts, body, init)

    zero = jnp.zeros((1, C), F32)
    sums = fold(lambda n, a: a + jnp.sum(frame_rows(n), axis=0, keepdims=True), zero)
    mean = group_sum(sums, member) / (entries * R)

    def deviation(n, a):
        d = frame_rows(n) - mean
        return a + jnp.sum(d * d, axis=0, keepdims=True)

    var = group_sum(fold(deviation, zero), member) / (entries * R)
    scale3 = lax.rsqrt(var + EPS) * flat(g3)
    shift3 = flat(s3)

    def normalise(n, c):
        start = pl.multiple_of(n * chunk, 16)
        value = ((frame_rows(n) - mean) * scale3 + shift3).astype(BF16)
        normed[0, pl.ds(start, chunk), :] = value
        normed[1, pl.ds(start, chunk), :] = jnp.dot(value, aw[1], preferred_element_type=F32).astype(BF16)
        normed[2, pl.ds(start, chunk), :] = jnp.dot(value, aw[2], preferred_element_type=F32).astype(BF16)
        return c

    fold(normalise, 0)
    mine = pl.ds(pl.multiple_of(z * RP, 16), RP)
    queries = (jnp.dot(normed[0, mine, :], aw[0], preferred_element_type=F32) * C ** (-0.5)).astype(BF16)
    scores = lax.dot_general(queries, normed[1], NT, preferred_element_type=F32)
    peak = jnp.max(scores, axis=1, keepdims=True)
    weights = jnp.exp(scores - peak)
    total = jnp.sum(weights, axis=1, keepdims=True)
    summed = jnp.dot(weights.astype(BF16), normed[2], preferred_element_type=F32)
    attended = (summed / total).astype(BF16)
    hidden = joined([hfull[s, mine, :] for s in range(T)])
    out[...] = (hidden + jnp.dot(attended, aw[3], preferred_element_type=F32)).astype(BF16)

    each(N - 1, lambda n: hidden_copy(n).wait_send())


def solution(mesh):
    T, R = mesh.shape["tm"], mesh.shape["rows"]

    def per_device(features, g1, s1, k1, b1, g2, s2, k2, b2, g3, s3, wq, wk, wv, wo):
        _, rows, W, C = features.shape
        OUT = k1.shape[0]
        RP, EXT, N = rows * W, (rows + 2) * W, T * R
        taps = lambda k: jnp.transpose(k, (1, 2, 3, 0, 4)).reshape(27, OUT, C)
        vmem = pl.BlockSpec(memory_space=pltpu.VMEM)
        hbm = pl.BlockSpec(memory_space=pltpu.HBM)
        dma = pltpu.SemaphoreType.DMA
        result = pl.pallas_call(
            functools.partial(kernel, T, R, W, rows, C, OUT),
            out_shape=jax.ShapeDtypeStruct((RP, C), BF16),
            in_specs=[hbm] * 15,
            out_specs=vmem,
            scratch_shapes=[pltpu.VMEM((RP, C), BF16)] + [pltpu.VMEM((C,), F32)] * 6
            + [pltpu.VMEM((OUT,), F32)] * 2 + [
                pltpu.VMEM((T, EXT, C), BF16),
                pltpu.VMEM((T, T, EXT, LANES), BF16),
                pltpu.VMEM((T, EXT, 3 * C), BF16),
                pltpu.VMEM((27, LANES, C), BF16),
                pltpu.VMEM((27, LANES, C), BF16),
                pltpu.VMEM((4, C, C), BF16),
                pltpu.VMEM((N, 2, C), F32),
                pltpu.VMEM((N, 2, T, LANES), F32),
                pltpu.VMEM((T, RP, LANES), BF16),
                pltpu.VMEM((T, R * RP, LANES), BF16),
                pltpu.VMEM((3, R * RP, C), BF16),
                dma((15,)),
                dma((2, T)), dma((2, T)),
                dma((2, T)), dma((2, T)),
                dma((2, T)), dma((2, T)),
                dma((2, N)), dma((2, N)),
                dma((N,)), dma((N,)),
            ],
            compiler_params=pltpu.CompilerParams(
                collective_id=0, has_side_effects=True, vmem_limit_bytes=62 * 1024 * 1024),
        )(features.reshape(RP, C), g1, s1, taps(k1), b1, g2, s2,
          taps(k2), b2, g3, s3, wq, wk, wv, wo)
        return result.reshape(features.shape)

    in_specs = (
        P(("clips", "tm"), "rows", None, None), P(), P(),
        P("tm", None, None, None, None), P("tm"), P(), P(),
        P("tm", None, None, None, None), P("tm"), P(), P(), P(), P(), P(), P(),
    )
    return jax.shard_map(
        per_device, mesh=mesh, in_specs=in_specs,
        out_specs=P(("clips", "tm"), "rows", None, None), check_vma=False)
```
